512 devices in a mesh: dp: 32 (over z, core), ctx: 16 (over x, y).
Axes of the slice: x: 4, y: 4, z: 16, core: 2. Of those that a mesh axis runs over, the one named last changes fastest.
Arguments:
- queries: bfloat16 [65536, 2048], P(('dp', 'ctx')), may hold values from -120 to 120
- keys: bfloat16 [65536, 1024], P(('dp', 'ctx')), may hold values from -4 to 4
- values: bfloat16 [65536, 1024], P(('dp', 'ctx')), may hold values from -6 to 6
- grad_out: bfloat16 [65536, 2048], P(('dp', 'ctx')), may hold values from -6 to 6
- doc_lengths: int32 [128], replicated, may hold values from 1 to 1024, 65536 in all
Outputs:
- attended: bfloat16 [65536, 2048], P(('dp', 'ctx'))
- grad_queries: bfloat16 [65536, 2048], P(('dp', 'ctx'))
- grad_keys: bfloat16 [65536, 1024], P(('dp', 'ctx'))
- grad_values: bfloat16 [65536, 1024], P(('dp', 'ctx'))
The draws below stay inside these ranges and needn't reach their ends.
Inputs may be any that keep to these rules, and one draw needn't show every extreme that they name: doc_lengths lists 128 documents that fill all 65536 tokens in order; the longest has exactly 1024 tokens.
All inputs are finite; a program needn't handle non-finite values.
Results may differ from the reference program's by a relative error of at most 0.024.
Values may be sent and summed in bfloat16 or wider, within the bound.
No kernel may reach another device: no remote copies, remote signals or barrier semaphores. Data moves between devices by JAX's collectives and lax.ppermute only.
A program may use at most 128 MiB of HBM per device.

```python
import math
import jax
import jax.numpy as jnp
import numpy as np
from jax import lax

HEADS = 16
KV_HEADS = 8
HD = 128
LEN_MAX = 1024
TOKENS = 65536
DOCS = 128


def key_table(key, pull):
    base_keys = jnp.clip(jax.random.normal(jax.random.fold_in(key, 11), (TOKENS, KV_HEADS * HD), jnp.float32), -4.0, 4.0)
    offset = jax.random.randint(jax.random.fold_in(key, 12), (), 0, 67)
    row_index = jnp.arange(TOKENS, dtype=jnp.int32)
    chosen = ((row_index + offset) % 67 == 0) & (row_index >= 1)
    levels = jnp.array([18.0, 24.0, 30.0], jnp.float32)
    strength = levels[jax.random.randint(jax.random.fold_in(key, 13), (TOKENS,), 0, 3)]
    shrink = 1.0 - 24.0 / (strength * HD)
    before = jnp.roll(chosen, -1)
    nearby = jnp.roll(base_keys, -1, axis=0) * jnp.roll(shrink, -1)[:, None]
    table = jnp.where((before & (pull > 0.0))[:, None], nearby, base_keys)
    return table


def draw_keys(key, part):
    table = key_table(key, 0.0)
    return table.astype(jnp.bfloat16)


def draw_queries(key, part):
    key = jax.random.fold_in(key, 5)
    drawn = 3.0 * jnp.clip(jax.random.normal(key, (TOKENS, HEADS * HD), jnp.float32), -6.0, 6.0)
    return drawn.astype(jnp.bfloat16)


def block_scale(own_key, shape, split, low, largest):
    loudness, own = 1.0, jax.random.fold_in(own_key, 6)
    for position, shards_of in split:
        steps = jnp.exp(jax.random.uniform(jax.random.fold_in(own, position), (shards_of,), jnp.float32, low / len(split), largest / len(split)))
        loudness = loudness * jnp.repeat(steps, shape[position] // shards_of).reshape([-1 if axis == position else 1 for axis in range(len(shape))])
    return loudness


def length_profile(amount, total, reach, lean):
    portions = [(1 << 20) // math.isqrt(rank ** lean) + 1 for rank in range(2, amount + 1)]
    spare, holding = total - reach - (amount - 1), [1] * (amount - 1)
    while spare > 0:
        movable = [i for i in range(amount - 1) if holding[i] < reach]
        pool, remaining = sum([portions[i] for i in movable]), spare
        for i in movable:
            addition = min(reach - holding[i], max(1, remaining * portions[i] // pool), spare)
            holding[i] = holding[i] + addition
            spare = spare - addition
    return np.array([reach] + holding)


def uneven_parts(key, count, total, limit, lean):
    if count == 2:
        one = jax.random.randint(key, (), max(1, total - limit), min(limit, total - 1) + 1)
        return jnp.stack([one, total - one])
    sizes = jnp.asarray(length_profile(count, total, limit, lean), jnp.int32)
    twos = (count - 1) // 2
    donor, taker = sizes[1:1 + 2 * twos:2], sizes[2:2 + 2 * twos:2]
    room = jnp.minimum(donor - 1, limit - taker)
    shifted = jax.random.randint(jax.random.fold_in(key, 1), (twos,), 0, 1 << 20) % (room + 1)
    sizes = sizes.at[1:1 + 2 * twos:2].set(donor - shifted).at[2:2 + 2 * twos:2].set(taker + shifted)
    return sizes[jax.random.permutation(jax.random.fold_in(key, 2), count)]


def scatter_about(key, shape, deviation, limit, pieces=(), kind=jnp.bfloat16):
    level = block_scale(key, shape, pieces, -0.22, 0.18) if pieces else 1.0
    values = jax.random.normal(key, shape, jnp.float32) * deviation * level
    return jnp.minimum(jnp.maximum(values, -limit), limit).astype(kind)


def setup_inputs(seed: int = 0) -> dict:
    streams_of = jax.random.split(jax.random.key(seed), 6)
    return {
        "queries": draw_queries(jax.random.fold_in(streams_of[5], 71), 0),
        "keys": draw_keys(jax.random.fold_in(streams_of[5], 71), 0),
        "values": scatter_about(streams_of[2], (TOKENS, KV_HEADS * HD), 1.0, 6.0, ((0, 512),)),
        "grad_out": scatter_about(streams_of[3], (TOKENS, HEADS * HD), 1.0, 6.0, ((0, 512),)),
        "doc_lengths": uneven_parts(streams_of[4], DOCS, TOKENS, LEN_MAX, 2).astype(jnp.int32),
    }


q_scale = 144.0 ** -0.5
far_below = -1.0e30


def doc_ids(doc_lengths, positions):
    ends = jnp.cumsum(doc_lengths).astype(jnp.int32)
    found = jnp.sum((ends[None, :] <= positions[:, None]).astype(jnp.int32), axis=1)
    return jnp.where(positions >= 0, found, -1).astype(jnp.int32)


def masked_scores(q_part, k_part, ids_q, ids_k, pos_q, pos_k):
    scores = jnp.einsum("qhd,khd->hqk", q_part.astype(jnp.float32), k_part.astype(jnp.float32)) * q_scale
    allowed = (ids_q[:, None] == ids_k[None, :]) & (pos_k[None, :] <= pos_q[:, None])
    return jnp.where(allowed[None], scores, far_below)


def reference(queries, keys, values, grad_out, doc_lengths):
    block_len = LEN_MAX // 2
    block_count = TOKENS // block_len
    pad_len = 2 * block_len
    group_size = HEADS // KV_HEADS
    q_all = queries.reshape(TOKENS, HEADS, HD)
    d_all = grad_out.reshape(TOKENS, HEADS, HD)
    k_all = jnp.repeat(keys.reshape(TOKENS, KV_HEADS, HD), group_size, axis=1)
    v_all = jnp.repeat(values.reshape(TOKENS, KV_HEADS, HD), group_size, axis=1)
    zero_rows = jnp.zeros((pad_len, HEADS, HD), jnp.bfloat16)
    k_front = jnp.concatenate([zero_rows, k_all], axis=0)
    v_front = jnp.concatenate([zero_rows, v_all], axis=0)
    ids_front = doc_ids(doc_lengths, jnp.arange(-pad_len, TOKENS, dtype=jnp.int32))

    def forward(block_index):
        start_row = (block_index * block_len).astype(jnp.int32)
        q_part = lax.dynamic_slice_in_dim(q_all, start_row, block_len, 0)
        k_part = lax.dynamic_slice_in_dim(k_front, start_row, 3 * block_len, 0)
        v_part = lax.dynamic_slice_in_dim(v_front, start_row, 3 * block_len, 0)
        ids_q = lax.dynamic_slice_in_dim(ids_front, start_row + pad_len, block_len, 0)
        ids_k = lax.dynamic_slice_in_dim(ids_front, start_row, 3 * block_len, 0)
        pos_q = start_row + jnp.arange(block_len, dtype=jnp.int32)
        pos_k = start_row - pad_len + jnp.arange(3 * block_len, dtype=jnp.int32)
        scores = masked_scores(q_part, k_part, ids_q, ids_k, pos_q, pos_k)
        highest = jnp.max(scores, axis=2, keepdims=True)
        log_total = highest + jnp.log(jnp.sum(jnp.exp(scores - highest), axis=2, keepdims=True))
        weights = jnp.exp(scores - log_total)
        weights_b = lax.optimization_barrier(weights.astype(jnp.bfloat16))
        mixture = jnp.einsum("hqk,khd->qhd", weights_b.astype(jnp.float32), v_part.astype(jnp.float32))
        return mixture.astype(jnp.bfloat16), log_total[:, :, 0]

    attended, log_total = lax.map(forward, jnp.arange(block_count, dtype=jnp.int32))
    attended = attended.reshape(TOKENS, HEADS, HD)
    log_total = jnp.transpose(log_total, (1, 0, 2)).reshape(HEADS, TOKENS)
    row_delta = jnp.sum(d_all.astype(jnp.float32) * attended.astype(jnp.float32), axis=2)

    def query_grads(block_index):
        start_row = (block_index * block_len).astype(jnp.int32)
        q_part = lax.dynamic_slice_in_dim(q_all, start_row, block_len, 0)
        d_part = lax.dynamic_slice_in_dim(d_all, start_row, block_len, 0)
        k_part = lax.dynamic_slice_in_dim(k_front, start_row, 3 * block_len, 0)
        v_part = lax.dynamic_slice_in_dim(v_front, start_row, 3 * block_len, 0)
        ids_q = lax.dynamic_slice_in_dim(ids_front, start_row + pad_len, block_len, 0)
        ids_k = lax.dynamic_slice_in_dim(ids_front, start_row, 3 * block_len, 0)
        pos_q = start_row + jnp.arange(block_len, dtype=jnp.int32)
        pos_k = start_row - pad_len + jnp.arange(3 * block_len, dtype=jnp.int32)
        delta_part = lax.dynamic_slice_in_dim(row_delta, start_row, block_len, 0)
        total_part = lax.dynamic_slice_in_dim(log_total, start_row, block_len, 1)
        scores = masked_scores(q_part, k_part, ids_q, ids_k, pos_q, pos_k)
        weights = jnp.exp(scores - total_part[:, :, None])
        dprob = jnp.einsum("qhd,khd->hqk", d_part.astype(jnp.float32), v_part.astype(jnp.float32))
        dscore = weights * (dprob - jnp.transpose(delta_part)[:, :, None])
        dscore_b = lax.optimization_barrier(dscore.astype(jnp.bfloat16))
        grad_q = jnp.einsum("hqk,khd->qhd", dscore_b.astype(jnp.float32), k_part.astype(jnp.float32)) * q_scale
        return grad_q.astype(jnp.bfloat16)

    grad_queries = lax.map(query_grads, jnp.arange(block_count, dtype=jnp.int32)).reshape(TOKENS, HEADS * HD)

    q_back = jnp.concatenate([q_all, zero_rows], axis=0)
    d_back = jnp.concatenate([d_all, zero_rows], axis=0)
    delta_back = jnp.concatenate([row_delta, jnp.zeros((pad_len, HEADS), jnp.float32)], axis=0)
    total_back = jnp.concatenate([log_total, jnp.zeros((HEADS, pad_len), jnp.float32)], axis=1)
    ids_back = doc_ids(doc_lengths, jnp.arange(TOKENS + pad_len, dtype=jnp.int32))

    def key_grads(block_index):
        start_row = (block_index * block_len).astype(jnp.int32)
        k_part = lax.dynamic_slice_in_dim(k_all, start_row, block_len, 0)
        v_part = lax.dynamic_slice_in_dim(v_all, start_row, block_len, 0)
        q_part = lax.dynamic_slice_in_dim(q_back, start_row, 3 * block_len, 0)
        d_part = lax.dynamic_slice_in_dim(d_back, start_row, 3 * block_len, 0)
        delta_part = lax.dynamic_slice_in_dim(delta_back, start_row, 3 * block_len, 0)
        total_part = lax.dynamic_slice_in_dim(total_back, start_row, 3 * block_len, 1)
        ids_k = lax.dynamic_slice_in_dim(ids_back, start_row, block_len, 0)
        ids_q = lax.dynamic_slice_in_dim(ids_back, start_row, 3 * block_len, 0)
        pos_k = start_row + jnp.arange(block_len, dtype=jnp.int32)
        pos_q = start_row + jnp.arange(3 * block_len, dtype=jnp.int32)
        scores = masked_scores(q_part, k_part, ids_q, ids_k, pos_q, pos_k)
        weights = jnp.exp(scores - total_part[:, :, None])
        weights_b = lax.optimization_barrier(weights.astype(jnp.bfloat16))
        dprob = jnp.einsum("qhd,khd->hqk", d_part.astype(jnp.float32), v_part.astype(jnp.float32))
        dscore = weights * (dprob - jnp.transpose(delta_part)[:, :, None])
        dscore_b = lax.optimization_barrier(dscore.astype(jnp.bfloat16))
        grad_k = jnp.einsum("hqk,qhd->khd", dscore_b.astype(jnp.float32), q_part.astype(jnp.float32)) * q_scale
        grad_v = jnp.einsum("hqk,qhd->khd", weights_b.astype(jnp.float32), d_part.astype(jnp.float32))
        grad_k = jnp.sum(grad_k.reshape(block_len, KV_HEADS, group_size, HD), axis=2)
        grad_v = jnp.sum(grad_v.reshape(block_len, KV_HEADS, group_size, HD), axis=2)
        return grad_k.astype(jnp.bfloat16), grad_v.astype(jnp.bfloat16)

    grad_keys, grad_values = lax.map(key_grads, jnp.arange(block_count, dtype=jnp.int32))
    grad_keys = grad_keys.reshape(TOKENS, KV_HEADS * HD)
    grad_values = grad_values.reshape(TOKENS, KV_HEADS * HD)
    return attended.reshape(TOKENS, HEADS * HD), grad_queries, grad_keys, grad_values
```

```python
import jax
import jax.numpy as jnp
from jax import lax
from jax.experimental import pallas as pl
from jax.experimental.pallas import tpu as pltpu
from jax.sharding import PartitionSpec as P

HEADS = 16
KV_HEADS = 8
HD = 128
GROUP = HEADS // KV_HEADS

TOK = 128
PEERS = 8
HALF = TOK * PEERS
BLK = 256
HALF_BLKS = HALF // BLK
PAIR = BLK // TOK
COLS = GROUP * BLK

q_scale = 144.0 ** (-0.5)
log2_e = 1.4426950408889634
far_below = -1e30

OWNERS = ((0, 1, 2, 3, 4, 5, 6, 7), (12, 13, 14, 15, 8, 9, 10, 11))


def exchange(array):
    return lax.all_to_all(
        array, "ctx", split_axis=0, concat_axis=0, tiled=True, axis_index_groups=[list(g) for g in OWNERS]
    )


def next_half_pairs(rows):
    pairs = []
    for row in range(rows):
        for first, second in zip(*OWNERS):
            pairs.append((row * 16 + first, row * 16 + second))
            if row + 1 < rows:
                pairs.append((row * 16 + second, (row + 1) * 16 + first))
    return pairs


def nt(left, right):
    return lax.dot_general(left, right, (((1,), (1,)), ((), ())), preferred_element_type=jnp.float32)


def nn(left, right):
    return lax.dot_general(left, right, (((1,), (0,)), ((), ())), preferred_element_type=jnp.float32)


def fold(array, op):
    return op(array.reshape(BLK // 8, 8, COLS), axis=0)


def attend_kernel(
    info, qd, kv, halo, starts, od, own_grads, halo_grads,
    k_rows, v_rows, k_cols, v_cols, held, key_grads, value_grads,
):
    half = info[0]

    def own_at(block):
        return lax.rem(block + half * (HALF_BLKS // 2), HALF_BLKS) * PAIR

    def halo_at(block):
        return lax.rem(block + (1 - half) * (HALF_BLKS // 2), HALF_BLKS) * PAIR

    for block in range(HALF_BLKS):
        for ref, at, first in ((halo, halo_at, 0), (kv, own_at, HALF)):
            rows = pl.ds(first + block * BLK, BLK)
            k_blk = ref[pl.ds(at(block), PAIR), 0].reshape(BLK, HD)
            v_blk = ref[pl.ds(at(block), PAIR), 1].reshape(BLK, HD)
            k_rows[rows, :] = k_blk
            v_rows[rows, :] = v_blk
            k_cols[:, rows] = k_blk.T
            v_cols[:, rows] = v_blk.T
    key_grads[...] = jnp.zeros_like(key_grads)
    value_grads[...] = jnp.zeros_like(value_grads)

    for block in range(HALF_BLKS):
        q_at = pl.ds(own_at(block), PAIR)
        q_blk = jnp.concatenate([qd[q_at, 0].reshape(BLK, HD), qd[q_at, 1].reshape(BLK, HD)], axis=0)
        d_blk = jnp.concatenate([qd[q_at, 2].reshape(BLK, HD), qd[q_at, 3].reshape(BLK, HD)], axis=0)
        q_cols = q_blk.T
        d_cols = d_blk.T
        start = starts[block]
        low = info[1 + block]
        diag = HALF_BLKS + block

        def score(key_block, causal):
            rows = pl.ds(pl.multiple_of(key_block * BLK, BLK), BLK)
            piece = nn(k_rows[rows, :], q_cols)
            at = lax.broadcasted_iota(jnp.int32, (BLK, COLS), 0)
            allowed = at >= start - key_block * BLK
            if causal:
                q_pos = lax.rem(lax.broadcasted_iota(jnp.int32, (BLK, COLS), 1), BLK)
                allowed = allowed & (at <= q_pos)
            piece = jnp.where(allowed, piece, far_below)
            held[key_block - block] = piece
            return fold(piece, jnp.max)

        highest = score(diag, True)
        highest = lax.fori_loop(
            low, diag, lambda key_block, best: jnp.maximum(best, score(key_block, False)), highest
        )
        highest = jnp.max(highest, axis=0, keepdims=True) * (q_scale * log2_e)

        def weigh(key_block, carry):
            summed, mixture = carry
            rows = pl.ds(pl.multiple_of(key_block * BLK, BLK), BLK)
            piece = jnp.exp2(held[key_block - block] * (q_scale * log2_e) - highest)
            held[key_block - block] = piece
            summed = summed + fold(piece, jnp.sum)
            mixture = mixture + nn(v_cols[:, rows], piece.astype(jnp.bfloat16))
            return summed, mixture

        summed, mixture = lax.fori_loop(
            low, diag + 1, weigh, (jnp.zeros((8, COLS), jnp.float32), jnp.zeros((HD, COLS), jnp.float32))
        )
        inverse = 1.0 / jnp.sum(summed, axis=0, keepdims=True)
        attended = (mixture * inverse).astype(jnp.bfloat16)
        row_delta = jnp.sum(
            attended.astype(jnp.float32) * d_cols.astype(jnp.float32), axis=0, keepdims=True
        )
        out_rows = attended.T
        od[q_at, 0] = out_rows[:BLK].reshape(PAIR, TOK, HD)
        od[q_at, 1] = out_rows[BLK:].reshape(PAIR, TOK, HD)

        def spread(key_block, grad_q):
            rows = pl.ds(pl.multiple_of(key_block * BLK, BLK), BLK)
            weights = held[key_block - block] * inverse
            dscore = (weights * (nn(v_rows[rows, :], d_cols) - row_delta)).astype(jnp.bfloat16)
            value_grads[rows, :] += nn(weights.astype(jnp.bfloat16), d_blk)
            key_grads[rows, :] += nn(dscore, q_blk)
            return grad_q + nn(k_cols[:, rows], dscore)

        grad_q = lax.fori_loop(low, diag + 1, spread, jnp.zeros((HD, COLS), jnp.float32))
        out_rows = (grad_q * q_scale).astype(jnp.bfloat16).T
        od[q_at, 2] = out_rows[:BLK].reshape(PAIR, TOK, HD)
        od[q_at, 3] = out_rows[BLK:].reshape(PAIR, TOK, HD)

    for block in range(HALF_BLKS):
        for ref, at, first in ((halo_grads, halo_at, 0), (own_grads, own_at, HALF)):
            rows = pl.ds(first + block * BLK, BLK)
            at_pair = pl.ds(at(block), PAIR)
            ref[at_pair, 0] = (key_grads[rows, :] * q_scale).astype(ref.dtype).reshape(PAIR, TOK, HD)
            ref[at_pair, 1] = value_grads[rows, :].astype(ref.dtype).reshape(PAIR, TOK, HD)


def attend_half(info, qd, kv, halo, starts):
    in_vmem = pl.BlockSpec(memory_space=pltpu.VMEM)
    return pl.pallas_call(
        attend_kernel,
        out_shape=(
            jax.ShapeDtypeStruct((PEERS, 2 * GROUP, TOK, HD), jnp.bfloat16),
            jax.ShapeDtypeStruct((PEERS, 2, TOK, HD), jnp.float32),
            jax.ShapeDtypeStruct((PEERS, 2, TOK, HD), jnp.bfloat16),
        ),
        in_specs=[pl.BlockSpec(memory_space=pltpu.SMEM)] + [in_vmem] * 4,
        out_specs=(in_vmem, in_vmem, in_vmem),
        scratch_shapes=[
            pltpu.VMEM((2 * HALF, HD), jnp.bfloat16),
            pltpu.VMEM((2 * HALF, HD), jnp.bfloat16),
            pltpu.VMEM((HD, 2 * HALF), jnp.bfloat16),
            pltpu.VMEM((HD, 2 * HALF), jnp.bfloat16),
            pltpu.VMEM((HALF_BLKS + 1, BLK, COLS), jnp.float32),
            pltpu.VMEM((2 * HALF, HD), jnp.float32),
            pltpu.VMEM((2 * HALF, HD), jnp.float32),
        ],
        compiler_params=pltpu.CompilerParams(vmem_limit_bytes=40 * 1024 * 1024),
        name="attend_half",
    )(info, qd, kv, halo, starts)


def doc_reach(doc_lengths, half_index):
    before = lax.broadcasted_iota(jnp.int32, (128, 128), 0) <= lax.broadcasted_iota(jnp.int32, (128, 128), 1)
    ends = jnp.sum(jnp.where(before, doc_lengths[:, None], 0), axis=0)
    positions = half_index * HALF + jnp.arange(HALF, dtype=jnp.int32)
    begins = jnp.max(jnp.where(ends[None, :] <= positions[:, None], ends[None, :], 0), axis=1)
    begins = (begins - (half_index - 1) * HALF).reshape(HALF_BLKS, 1, BLK)
    low = begins[:, 0, 0] // BLK
    return jnp.concatenate([begins] * GROUP, axis=2), low


def packed(first, second, width):
    first = first.reshape(TOK, PEERS, width, HD)
    second = second.reshape(TOK, PEERS, width, HD)
    return jnp.concatenate([first, second], axis=2).transpose(1, 2, 0, 3)


def unpacked(array, width):
    array = array.transpose(2, 0, 1, 3)
    return (
        array[:, :, :width].reshape(TOK, PEERS * width * HD),
        array[:, :, width:].reshape(TOK, PEERS * width * HD),
    )


def on_device(queries, keys, values, grad_out, doc_lengths):
    ahead = next_half_pairs(lax.axis_size("dp"))
    behind = [(to, of) for of, to in ahead]
    both = ("dp", "ctx")
    half = lax.axis_index("ctx") // PEERS
    starts, low = doc_reach(doc_lengths, lax.axis_index("dp") * 2 + half)
    info = jnp.concatenate([half[None].astype(jnp.int32), low])

    kv = exchange(packed(keys, values, 1))
    halo = lax.ppermute(kv, both, ahead)
    qd = exchange(packed(queries, grad_out, GROUP))
    od, own_grads, halo_grads = attend_half(info, qd, kv, halo, starts)
    back = lax.ppermute(halo_grads, both, behind)
    attended, grad_queries = unpacked(exchange(od), GROUP)
    grads = (own_grads + back.astype(jnp.float32)).astype(jnp.bfloat16)
    grad_keys, grad_values = unpacked(exchange(grads), 1)
    return attended, grad_queries, grad_keys, grad_values


def solution(mesh):
    rows = P(("dp", "ctx"), None)
    return jax.shard_map(
        on_device, mesh=mesh, in_specs=(rows, rows, rows, rows, P()), out_specs=(rows,) * 4, check_vma=False
    )
```

```python
import functools

import jax
import jax.numpy as jnp
from jax import lax
from jax.experimental import pallas as pl
from jax.experimental.pallas import tpu as pltpu
from jax.sharding import PartitionSpec as P

HEADS = 16
KV_HEADS = 8
HD = 128
GROUP = HEADS // KV_HEADS

TOK = 128
PEERS = 8
HALF = TOK * PEERS
BLK = 256
HALF_BLKS = HALF // BLK
PAIR = BLK // TOK
COLS = GROUP * BLK

q_scale = 144.0 ** (-0.5)
log2_e = 1.4426950408889634
far_below = -1e30

OWNERS = ((0, 1, 2, 3, 4, 5, 6, 7), (12, 13, 14, 15, 8, 9, 10, 11))


def exchange(array):
    return lax.all_to_all(
        array, "ctx", split_axis=0, concat_axis=0, tiled=True, axis_index_groups=[list(g) for g in OWNERS]
    )


def next_half_pairs(rows):
    pairs = []
    for row in range(rows):
        for first, second in zip(*OWNERS):
            pairs.append((row * 16 + first, row * 16 + second))
            if row + 1 < rows:
                pairs.append((row * 16 + second, (row + 1) * 16 + first))
    return pairs


def nt(left, right):
    return lax.dot_general(left, right, (((1,), (1,)), ((), ())), preferred_element_type=jnp.float32)


def nn(left, right):
    return lax.dot_general(left, right, (((1,), (0,)), ((), ())), preferred_element_type=jnp.float32)


def fold(array, op):
    return op(array.reshape(BLK // 8, 8, COLS), axis=0)


def attend_kernel(
    info, qd, kv, halo, starts, out_cols, own_grads, halo_grads,
    k_rows, v_rows, k_cols, v_cols, held, key_grads, value_grads,
):
    half = info[0]

    def own_at(block):
        return lax.rem(block + half * (HALF_BLKS // 2), HALF_BLKS) * PAIR

    def halo_at(block):
        return lax.rem(block + (1 - half) * (HALF_BLKS // 2), HALF_BLKS) * PAIR

    for block in range(HALF_BLKS):
        for ref, at, first in ((halo, halo_at, 0), (kv, own_at, HALF_BLKS)):
            k_blk = ref[pl.ds(at(block), PAIR), 0].reshape(BLK, HD)
            v_blk = ref[pl.ds(at(block), PAIR), 1].reshape(BLK, HD)
            k_rows[first + block] = k_blk
            v_rows[first + block] = v_blk
            k_cols[first + block] = k_blk.T
            v_cols[first + block] = v_blk.T
    key_grads[...] = jnp.zeros_like(key_grads)
    value_grads[...] = jnp.zeros_like(value_grads)

    def attend(block, count):
        q_at = pl.ds(own_at(block), PAIR)
        q_blk = jnp.concatenate([qd[q_at, 0].reshape(BLK, HD), qd[q_at, 1].reshape(BLK, HD)], axis=0)
        d_blk = jnp.concatenate([qd[q_at, 2].reshape(BLK, HD), qd[q_at, 3].reshape(BLK, HD)], axis=0)
        q_cols = q_blk.T
        d_cols = d_blk.T
        start = starts[block]
        low = HALF_BLKS + block + 1 - count
        highest = None
        for step in range(count):
            piece = nn(k_rows[low + step], q_cols)
            at = lax.broadcasted_iota(jnp.int32, (BLK, COLS), 0)
            allowed = at >= start - (low + step) * BLK
            if step == count - 1:
                q_pos = lax.rem(lax.broadcasted_iota(jnp.int32, (BLK, COLS), 1), BLK)
                allowed = allowed & (at <= q_pos)
            piece = jnp.where(allowed, piece, far_below)
            held[step] = piece
            best = fold(piece, jnp.max)
            highest = best if highest is None else jnp.maximum(highest, best)
        highest = jnp.max(highest, axis=0, keepdims=True) * (q_scale * log2_e)
        summed = mixture = 0.0
        for step in range(count):
            piece = jnp.exp2(held[step] * (q_scale * log2_e) - highest)
            held[step] = piece
            summed = summed + fold(piece, jnp.sum)
            mixture = mixture + nn(v_cols[low + step], piece.astype(jnp.bfloat16))
        inverse = 1.0 / jnp.sum(summed, axis=0, keepdims=True)
        attended = (mixture * inverse).astype(jnp.bfloat16)
        row_delta = jnp.sum(
            attended.astype(jnp.float32) * d_cols.astype(jnp.float32), axis=0, keepdims=True
        )
        out_cols[block, 0] = attended
        grad_q = 0.0
        for step in range(count):
            weights = held[step] * inverse
            dscore = (weights * (nn(v_rows[low + step], d_cols) - row_delta)).astype(jnp.bfloat16)
            value_grads[low + step] += nn(weights.astype(jnp.bfloat16), d_blk)
            key_grads[low + step] += nn(dscore, q_blk)
            grad_q = grad_q + nn(k_cols[low + step], dscore)
        out_cols[block, 1] = (grad_q * q_scale).astype(jnp.bfloat16)

    @pl.loop(0, HALF_BLKS)
    def _(block):
        count = HALF_BLKS + block + 1 - info[1 + block]
        for choice in range(1, HALF_BLKS + 2):
            pl.when(count == choice)(lambda choice=choice: attend(block, choice))

    for block in range(HALF_BLKS):
        for ref, at, first in ((halo_grads, halo_at, 0), (own_grads, own_at, HALF_BLKS)):
            at_pair = pl.ds(at(block), PAIR)
            ref[at_pair, 0] = (key_grads[first + block] * q_scale).astype(ref.dtype).reshape(PAIR, TOK, HD)
            ref[at_pair, 1] = value_grads[first + block].astype(ref.dtype).reshape(PAIR, TOK, HD)


def attend_half(info, qd, kv, halo, starts):
    in_vmem = pl.BlockSpec(memory_space=pltpu.VMEM)
    return pl.pallas_call(
        attend_kernel,
        out_shape=(
            jax.ShapeDtypeStruct((HALF_BLKS, 2, HD, COLS), jnp.bfloat16),
            jax.ShapeDtypeStruct((PEERS, 2, TOK, HD), jnp.float32),
            jax.ShapeDtypeStruct((PEERS, 2, TOK, HD), jnp.bfloat16),
        ),
        in_specs=[pl.BlockSpec(memory_space=pltpu.SMEM)] + [in_vmem] * 4,
        out_specs=(in_vmem, in_vmem, in_vmem),
        scratch_shapes=[
            pltpu.VMEM((2 * HALF_BLKS, BLK, HD), jnp.bfloat16),
            pltpu.VMEM((2 * HALF_BLKS, BLK, HD), jnp.bfloat16),
            pltpu.VMEM((2 * HALF_BLKS, HD, BLK), jnp.bfloat16),
            pltpu.VMEM((2 * HALF_BLKS, HD, BLK), jnp.bfloat16),
            pltpu.VMEM((HALF_BLKS + 1, BLK, COLS), jnp.float32),
            pltpu.VMEM((2 * HALF_BLKS, BLK, HD), jnp.float32),
            pltpu.VMEM((2 * HALF_BLKS, BLK, HD), jnp.float32),
        ],
        compiler_params=pltpu.CompilerParams(vmem_limit_bytes=40 * 1024 * 1024),
        name="attend_half",
    )(info, qd, kv, halo, starts)


def doc_reach(doc_lengths, half_index):
    before = lax.broadcasted_iota(jnp.int32, (128, 128), 0) <= lax.broadcasted_iota(jnp.int32, (128, 128), 1)
    ends = jnp.sum(jnp.where(before, doc_lengths[:, None], 0), axis=0)
    positions = half_index * HALF + jnp.arange(HALF, dtype=jnp.int32)
    begins = jnp.max(jnp.where(ends[None, :] <= positions[:, None], ends[None, :], 0), axis=1)
    begins = (begins - (half_index - 1) * HALF).reshape(HALF_BLKS, 1, BLK)
    low = begins[:, 0, 0] // BLK
    return jnp.concatenate([begins] * GROUP, axis=2), low


def turn_kernel(info, out_cols, od):
    for block in range(HALF_BLKS):
        at = pl.ds(lax.rem(block + info[0] * (HALF_BLKS // 2), HALF_BLKS) * PAIR, PAIR)
        for kind in range(2):
            rows = out_cols[block, kind].T
            for head in range(GROUP):
                od[at, kind * GROUP + head] = rows[head * BLK : (head + 1) * BLK].reshape(PAIR, TOK, HD)


def turned(info, out_cols):
    in_vmem = pl.BlockSpec(memory_space=pltpu.VMEM)
    return pl.pallas_call(
        turn_kernel,
        out_shape=jax.ShapeDtypeStruct((PEERS, 2 * GROUP, TOK, HD), jnp.bfloat16),
        in_specs=[pl.BlockSpec(memory_space=pltpu.SMEM), in_vmem],
        out_specs=in_vmem,
        name="turn_outputs",
    )(info, out_cols)


def pieces(width):
    for peer in range(PEERS):
        for place in range(width):
            yield peer, place, pl.ds((peer * width + place) * HD, HD)


def pack_kernel(width, first, second, out):
    for peer, place, columns in pieces(width):
        out[peer, place] = first[:, columns]
        out[peer, width + place] = second[:, columns]


def packed(first, second, width):
    in_vmem = pl.BlockSpec(memory_space=pltpu.VMEM)
    return pl.pallas_call(
        functools.partial(pack_kernel, width),
        out_shape=jax.ShapeDtypeStruct((PEERS, 2 * width, TOK, HD), jnp.bfloat16),
        in_specs=[in_vmem, in_vmem],
        out_specs=in_vmem,
        name="pack_heads",
    )(first, second)


def unpack_kernel(width, array, first, second):
    for peer, place, columns in pieces(width):
        first[:, columns] = array[peer, place]
        second[:, columns] = array[peer, width + place]


def unpacked(array, width):
    in_vmem = pl.BlockSpec(memory_space=pltpu.VMEM)
    rows = jax.ShapeDtypeStruct((TOK, PEERS * width * HD), jnp.bfloat16)
    return pl.pallas_call(
        functools.partial(unpack_kernel, width),
        out_shape=(rows, rows),
        in_specs=[in_vmem],
        out_specs=(in_vmem, in_vmem),
        name="unpack_heads",
    )(array)


def on_device(queries, keys, values, grad_out, doc_lengths):
    ahead = next_half_pairs(lax.axis_size("dp"))
    behind = [(to, of) for of, to in ahead]
    both = ("dp", "ctx")
    half = lax.axis_index("ctx") // PEERS
    starts, low = doc_reach(doc_lengths, lax.axis_index("dp") * 2 + half)
    info = jnp.concatenate([half[None].astype(jnp.int32), low])

    kv = exchange(packed(keys, values, 1))
    halo = lax.ppermute(kv, both, ahead)
    qd = exchange(packed(queries, grad_out, GROUP))
    out_cols, own_grads, halo_grads = attend_half(info, qd, kv, halo, starts)
    back = lax.ppermute(halo_grads, both, behind)
    od = turned(info, out_cols)
    attended, grad_queries = unpacked(exchange(od), GROUP)
    grads = (own_grads + back.astype(jnp.float32)).astype(jnp.bfloat16)
    grad_keys, grad_values = unpacked(exchange(grads), 1)
    return attended, grad_queries, grad_keys, grad_values


def solution(mesh):
    rows = P(("dp", "ctx"), None)
    return jax.shard_map(
        on_device, mesh=mesh, in_specs=(rows, rows, rows, rows, P()), out_specs=(rows,) * 4, check_vma=False
    )
```

```python
import functools

import jax
import jax.numpy as jnp
from jax import lax
from jax.experimental import pallas as pl
from jax.experimental.pallas import tpu as pltpu
from jax.sharding import PartitionSpec as P

HEADS = 16
KV_HEADS = 8
HD = 128
GROUP = HEADS // KV_HEADS

TOK = 128
PEERS = 8
HALF = TOK * PEERS
BLK = 256
HALF_BLKS = HALF // BLK
PAIR = BLK // TOK
COLS = GROUP * BLK

q_scale = 144.0 ** (-0.5)
log2_e = 1.4426950408889634
far_below = -1e30

OWNERS = ((0, 1, 2, 3, 4, 5, 6, 7), (12, 13, 14, 15, 8, 9, 10, 11))


def exchange(array):
    return lax.all_to_all(
        array, "ctx", split_axis=0, concat_axis=0, tiled=True, axis_index_groups=[list(g) for g in OWNERS]
    )


def next_half_pairs(rows):
    pairs = []
    for row in range(rows):
        for first, second in zip(*OWNERS):
            pairs.append((row * 16 + first, row * 16 + second))
            if row + 1 < rows:
                pairs.append((row * 16 + second, (row + 1) * 16 + first))
    return pairs


def nt(left, right):
    return lax.dot_general(left, right, (((1,), (1,)), ((), ())), preferred_element_type=jnp.float32)


def nn(left, right):
    return lax.dot_general(left, right, (((1,), (0,)), ((), ())), preferred_element_type=jnp.float32)


def fold(array, op):
    return op(array.reshape(BLK // 8, 8, COLS), axis=0)


def attend_kernel(
    info, qd, kv, halo, starts, od, own_grads, halo_grads,
    k_rows, v_rows, k_cols, v_cols, held, key_grads, value_grads,
):
    half = info[0]

    def own_at(block):
        return lax.rem(block + half * (HALF_BLKS // 2), HALF_BLKS) * PAIR

    def halo_at(block):
        return lax.rem(block + (1 - half) * (HALF_BLKS // 2), HALF_BLKS) * PAIR

    for block in range(HALF_BLKS):
        for ref, at, first in ((halo, halo_at, 0), (kv, own_at, HALF_BLKS)):
            k_blk = ref[pl.ds(at(block), PAIR), 0].reshape(BLK, HD)
            v_blk = ref[pl.ds(at(block), PAIR), 1].reshape(BLK, HD)
            k_rows[first + block] = k_blk
            v_rows[first + block] = v_blk
            k_cols[first + block] = k_blk.T
            v_cols[first + block] = v_blk.T
    key_grads[...] = jnp.zeros_like(key_grads)
    value_grads[...] = jnp.zeros_like(value_grads)

    def attend(block, count):
        q_at = pl.ds(own_at(block), PAIR)
        q_blk = jnp.concatenate([qd[q_at, 0].reshape(BLK, HD), qd[q_at, 1].reshape(BLK, HD)], axis=0)
        d_blk = jnp.concatenate([qd[q_at, 2].reshape(BLK, HD), qd[q_at, 3].reshape(BLK, HD)], axis=0)
        q_cols = q_blk.T
        d_cols = d_blk.T
        start = starts[block]
        low = HALF_BLKS + block + 1 - count
        highest = None
        for step in range(count):
            piece = nn(k_rows[low + step], q_cols)
            at = lax.broadcasted_iota(jnp.int32, (BLK, COLS), 0)
            allowed = at >= start - (low + step) * BLK
            if step == count - 1:
                q_pos = lax.rem(lax.broadcasted_iota(jnp.int32, (BLK, COLS), 1), BLK)
                allowed = allowed & (at <= q_pos)
            piece = jnp.where(allowed, piece, far_below)
            held[step] = piece
            best = fold(piece, jnp.max)
            highest = best if highest is None else jnp.maximum(highest, best)
        highest = jnp.max(highest, axis=0, keepdims=True) * (q_scale * log2_e)
        summed = mixture = 0.0
        for step in range(count):
            piece = jnp.exp2(held[step] * (q_scale * log2_e) - highest)
            held[step] = piece
            summed = summed + fold(piece, jnp.sum)
            mixture = mixture + nn(v_cols[low + step], piece.astype(jnp.bfloat16))
        inverse = 1.0 / jnp.sum(summed, axis=0, keepdims=True)
        attended = (mixture * inverse).astype(jnp.bfloat16)
        row_delta = jnp.sum(
            attended.astype(jnp.float32) * d_cols.astype(jnp.float32), axis=0, keepdims=True
        )
        out_rows = attended.T
        od[q_at, 0] = out_rows[:BLK].reshape(PAIR, TOK, HD)
        od[q_at, 1] = out_rows[BLK:].reshape(PAIR, TOK, HD)
        grad_q = 0.0
        for step in range(count):
            weights = held[step] * inverse
            dscore = (weights * (nn(v_rows[low + step], d_cols) - row_delta)).astype(jnp.bfloat16)
            value_grads[low + step] += nn(weights.astype(jnp.bfloat16), d_blk)
            key_grads[low + step] += nn(dscore, q_blk)
            grad_q = grad_q + nn(k_cols[low + step], dscore)
        out_rows = (grad_q * q_scale).astype(jnp.bfloat16).T
        od[q_at, 2] = out_rows[:BLK].reshape(PAIR, TOK, HD)
        od[q_at, 3] = out_rows[BLK:].reshape(PAIR, TOK, HD)

    @pl.loop(0, HALF_BLKS)
    def _(block):
        count = HALF_BLKS + block + 1 - info[1 + block]
        for choice in range(1, HALF_BLKS + 2):
            pl.when(count == choice)(lambda choice=choice: attend(block, choice))

    for block in range(HALF_BLKS):
        for ref, at, first in ((halo_grads, halo_at, 0), (own_grads, own_at, HALF_BLKS)):
            at_pair = pl.ds(at(block), PAIR)
            ref[at_pair, 0] = (key_grads[first + block] * q_scale).astype(ref.dtype).reshape(PAIR, TOK, HD)
            ref[at_pair, 1] = value_grads[first + block].astype(ref.dtype).reshape(PAIR, TOK, HD)


def attend_half(info, qd, kv, halo, starts):
    in_vmem = pl.BlockSpec(memory_space=pltpu.VMEM)
    return pl.pallas_call(
        attend_kernel,
        out_shape=(
            jax.ShapeDtypeStruct((PEERS, 2 * GROUP, TOK, HD), jnp.bfloat16),
            jax.ShapeDtypeStruct((PEERS, 2, TOK, HD), jnp.float32),
            jax.ShapeDtypeStruct((PEERS, 2, TOK, HD), jnp.bfloat16),
        ),
        in_specs=[pl.BlockSpec(memory_space=pltpu.SMEM)] + [in_vmem] * 4,
        out_specs=(in_vmem, in_vmem, in_vmem),
        scratch_shapes=[
            pltpu.VMEM((2 * HALF_BLKS, BLK, HD), jnp.bfloat16),
            pltpu.VMEM((2 * HALF_BLKS, BLK, HD), jnp.bfloat16),
            pltpu.VMEM((2 * HALF_BLKS, HD, BLK), jnp.bfloat16),
            pltpu.VMEM((2 * HALF_BLKS, HD, BLK), jnp.bfloat16),
            pltpu.VMEM((HALF_BLKS + 1, BLK, COLS), jnp.float32),
            pltpu.VMEM((2 * HALF_BLKS, BLK, HD), jnp.float32),
            pltpu.VMEM((2 * HALF_BLKS, BLK, HD), jnp.float32),
        ],
        compiler_params=pltpu.CompilerParams(vmem_limit_bytes=40 * 1024 * 1024),
        name="attend_half",
    )(info, qd, kv, halo, starts)


def doc_reach(doc_lengths, half_index):
    before = lax.broadcasted_iota(jnp.int32, (128, 128), 0) <= lax.broadcasted_iota(jnp.int32, (128, 128), 1)
    ends = jnp.sum(jnp.where(before, doc_lengths[:, None], 0), axis=0)
    positions = half_index * HALF + jnp.arange(HALF, dtype=jnp.int32)
    begins = jnp.max(jnp.where(ends[None, :] <= positions[:, None], ends[None, :], 0), axis=1)
    begins = (begins - (half_index - 1) * HALF).reshape(HALF_BLKS, 1, BLK)
    low = begins[:, 0, 0] // BLK
    return jnp.concatenate([begins] * GROUP, axis=2), low


def pieces(width):
    for peer in range(PEERS):
        for place in range(width):
            yield peer, place, pl.ds((peer * width + place) * HD, HD)


def pack_kernel(width, first, second, out):
    for peer, place, columns in pieces(width):
        out[peer, place] = first[:, columns]
        out[peer, width + place] = second[:, columns]


def packed(first, second, width):
    in_vmem = pl.BlockSpec(memory_space=pltpu.VMEM)
    return pl.pallas_call(
        functools.partial(pack_kernel, width),
        out_shape=jax.ShapeDtypeStruct((PEERS, 2 * width, TOK, HD), jnp.bfloat16),
        in_specs=[in_vmem, in_vmem],
        out_specs=in_vmem,
        compiler_params=pltpu.CompilerParams(vmem_limit_bytes=8 * 1024 * 1024) if width > 1 else None,
        name="pack_heads",
    )(first, second)


def unpack_kernel(width, array, first, second):
    for peer, place, columns in pieces(width):
        first[:, columns] = array[peer, place]
        second[:, columns] = array[peer, width + place]


def unpacked(array, width):
    in_vmem = pl.BlockSpec(memory_space=pltpu.VMEM)
    rows = jax.ShapeDtypeStruct((TOK, PEERS * width * HD), jnp.bfloat16)
    return pl.pallas_call(
        functools.partial(unpack_kernel, width),
        out_shape=(rows, rows),
        in_specs=[in_vmem],
        out_specs=(in_vmem, in_vmem),
        compiler_params=pltpu.CompilerParams(vmem_limit_bytes=8 * 1024 * 1024),
        name="unpack_heads",
    )(array)


def join_kernel(own, back, out):
    out[...] = (own[...] + back[...].astype(jnp.float32)).astype(jnp.bfloat16)


def joined(own, back):
    in_vmem = pl.BlockSpec(memory_space=pltpu.VMEM)
    return pl.pallas_call(
        join_kernel,
        out_shape=jax.ShapeDtypeStruct(back.shape, jnp.bfloat16),
        in_specs=[in_vmem, in_vmem],
        out_specs=in_vmem,
        compiler_params=pltpu.CompilerParams(vmem_limit_bytes=8 * 1024 * 1024),
        cost_estimate=pl.CostEstimate(flops=30_000_000_000, bytes_accessed=100_000_000, transcendentals=0),
        name="join_grads",
    )(own, back)


def on_device(queries, keys, values, grad_out, doc_lengths):
    ahead = next_half_pairs(lax.axis_size("dp"))
    behind = [(to, of) for of, to in ahead]
    both = ("dp", "ctx")
    half = lax.axis_index("ctx") // PEERS
    starts, low = doc_reach(doc_lengths, lax.axis_index("dp") * 2 + half)
    info = jnp.concatenate([half[None].astype(jnp.int32), low])

    kv = exchange(packed(keys, values, 1))
    halo = lax.ppermute(kv, both, ahead)
    qd = exchange(packed(queries, grad_out, GROUP))
    od, own_grads, halo_grads = attend_half(info, qd, kv, halo, starts)
    back = lax.ppermute(halo_grads, both, behind)
    attended, grad_queries = unpacked(exchange(od), GROUP)
    grads = joined(own_grads, back)
    grad_keys, grad_values = unpacked(exchange(grads), 1)
    return attended, grad_queries, grad_keys, grad_values


def solution(mesh):
    rows = P(("dp", "ctx"), None)
    return jax.shard_map(
        on_device, mesh=mesh, in_specs=(rows, rows, rows, rows, P()), out_specs=(rows,) * 4, check_vma=False
    )
```

```python
import functools

import jax
import jax.numpy as jnp
from jax import lax
from jax.experimental import pallas as pl
from jax.experimental.pallas import tpu as pltpu
from jax.sharding import PartitionSpec as P

HEADS = 16
KV_HEADS = 8
HD = 128
GROUP = HEADS // KV_HEADS

TOK = 128
PEERS = 8
HALF = TOK * PEERS
BLK = 256
HALF_BLKS = HALF // BLK
PAIR = BLK // TOK
COLS = GROUP * BLK

q_scale = 144.0 ** (-0.5)
log2_e = 1.4426950408889634
far_below = -1e30

OWNERS = ((0, 1, 2, 3, 4, 5, 6, 7), (12, 13, 14, 15, 8, 9, 10, 11))


def exchange(array):
    return lax.all_to_all(
        array, "ctx", split_axis=0, concat_axis=0, tiled=True, axis_index_groups=[list(g) for g in OWNERS]
    )


def next_half_pairs(rows):
    pairs = []
    for row in range(rows):
        for first, second in zip(*OWNERS):
            pairs.append((row * 16 + first, row * 16 + second))
            if row + 1 < rows:
                pairs.append((row * 16 + second, (row + 1) * 16 + first))
    return pairs


def nt(left, right):
    return lax.dot_general(left, right, (((1,), (1,)), ((), ())), preferred_element_type=jnp.float32)


def nn(left, right):
    return lax.dot_general(left, right, (((1,), (0,)), ((), ())), preferred_element_type=jnp.float32)


def fold(array, op):
    return op(array.reshape(BLK // 8, 8, COLS), axis=0)


def attend_kernel(
    info, qd, kv, halo, starts, od, own_grads, halo_grads,
    k_rows, v_rows, k_cols, v_cols, held, key_grads, value_grads, od_rows, halo_rows, od_sems, halo_sem,
):
    half = info[0]

    def own_at(block):
        return lax.rem(block + half * (HALF_BLKS // 2), HALF_BLKS) * PAIR

    def halo_at(block):
        return lax.rem(block + (1 - half) * (HALF_BLKS // 2), HALF_BLKS) * PAIR

    for block in range(HALF_BLKS):
        for ref, at, first in ((halo, halo_at, 0), (kv, own_at, HALF_BLKS)):
            k_blk = ref[pl.ds(at(block), PAIR), 0].reshape(BLK, HD)
            v_blk = ref[pl.ds(at(block), PAIR), 1].reshape(BLK, HD)
            k_rows[first + block] = k_blk
            v_rows[first + block] = v_blk
            k_cols[first + block] = k_blk.T
            v_cols[first + block] = v_blk.T
    key_grads[...] = jnp.zeros_like(key_grads)
    value_grads[...] = jnp.zeros_like(value_grads)

    def attend(block, count):
        q_at = pl.ds(own_at(block), PAIR)
        q_blk = jnp.concatenate([qd[q_at, 0].reshape(BLK, HD), qd[q_at, 1].reshape(BLK, HD)], axis=0)
        d_blk = jnp.concatenate([qd[q_at, 2].reshape(BLK, HD), qd[q_at, 3].reshape(BLK, HD)], axis=0)
        q_cols = q_blk.T
        d_cols = d_blk.T
        start = starts[block]
        low = HALF_BLKS + block + 1 - count
        highest = None
        for step in range(count):
            piece = nn(k_rows[low + step], q_cols)
            at = lax.broadcasted_iota(jnp.int32, (BLK, COLS), 0)
            allowed = at >= start - (low + step) * BLK
            if step == count - 1:
                q_pos = lax.rem(lax.broadcasted_iota(jnp.int32, (BLK, COLS), 1), BLK)
                allowed = allowed & (at <= q_pos)
            piece = jnp.where(allowed, piece, far_below)
            held[step] = piece
            best = fold(piece, jnp.max)
            highest = best if highest is None else jnp.maximum(highest, best)
        highest = jnp.max(highest, axis=0, keepdims=True) * (q_scale * log2_e)
        summed = mixture = 0.0
        for step in range(count):
            piece = jnp.exp2(held[step] * (q_scale * log2_e) - highest)
            held[step] = piece
            summed = summed + fold(piece, jnp.sum)
            mixture = mixture + nn(v_cols[low + step], piece.astype(jnp.bfloat16))
        inverse = 1.0 / jnp.sum(summed, axis=0, keepdims=True)
        attended = (mixture * inverse).astype(jnp.bfloat16)
        row_delta = jnp.sum(
            attended.astype(jnp.float32) * d_cols.astype(jnp.float32), axis=0, keepdims=True
        )
        out_rows = attended.T
        od_rows[block, :, 0] = out_rows[:BLK].reshape(PAIR, TOK, HD)
        od_rows[block, :, 1] = out_rows[BLK:].reshape(PAIR, TOK, HD)
        grad_q = 0.0
        for step in range(count):
            weights = held[step] * inverse
            dscore = (weights * (nn(v_rows[low + step], d_cols) - row_delta)).astype(jnp.bfloat16)
            value_grads[low + step] += nn(weights.astype(jnp.bfloat16), d_blk)
            key_grads[low + step] += nn(dscore, q_blk)
            grad_q = grad_q + nn(k_cols[low + step], dscore)
        out_rows = (grad_q * q_scale).astype(jnp.bfloat16).T
        od_rows[block, :, 2] = out_rows[:BLK].reshape(PAIR, TOK, HD)
        od_rows[block, :, 3] = out_rows[BLK:].reshape(PAIR, TOK, HD)

    def od_copy(block):
        return pltpu.make_async_copy(od_rows.at[block], od.at[pl.ds(own_at(block), PAIR)], od_sems.at[block])

    @pl.loop(0, HALF_BLKS)
    def _(block):
        count = HALF_BLKS + block + 1 - info[1 + block]
        for choice in range(1, HALF_BLKS + 2):
            pl.when(count == choice)(lambda choice=choice: attend(block, choice))
        od_copy(block).start()

    for block in range(HALF_BLKS):
        at_pair = pl.ds(halo_at(block), PAIR)
        halo_rows[at_pair, 0] = (key_grads[block] * q_scale).astype(jnp.bfloat16).reshape(PAIR, TOK, HD)
        halo_rows[at_pair, 1] = value_grads[block].astype(jnp.bfloat16).reshape(PAIR, TOK, HD)
    halo_copy = pltpu.make_async_copy(halo_rows, halo_grads, halo_sem)
    halo_copy.start()
    for block in range(HALF_BLKS):
        at_pair = pl.ds(own_at(block), PAIR)
        own_grads[at_pair, 0] = (key_grads[HALF_BLKS + block] * q_scale).reshape(PAIR, TOK, HD)
        own_grads[at_pair, 1] = value_grads[HALF_BLKS + block].reshape(PAIR, TOK, HD)
    for block in range(HALF_BLKS):
        od_copy(block).wait()
    halo_copy.wait()


def attend_half(info, qd, kv, halo, starts):
    in_vmem = pl.BlockSpec(memory_space=pltpu.VMEM)
    in_hbm = pl.BlockSpec(memory_space=pltpu.HBM)
    return pl.pallas_call(
        attend_kernel,
        out_shape=(
            pltpu.HBM((PEERS, 2 * GROUP, TOK, HD), jnp.bfloat16),
            jax.ShapeDtypeStruct((PEERS, 2, TOK, HD), jnp.float32),
            pltpu.HBM((PEERS, 2, TOK, HD), jnp.bfloat16),
        ),
        in_specs=[pl.BlockSpec(memory_space=pltpu.SMEM)] + [in_vmem] * 4,
        out_specs=(in_hbm, in_vmem, in_hbm),
        scratch_shapes=[
            pltpu.VMEM((2 * HALF_BLKS, BLK, HD), jnp.bfloat16),
            pltpu.VMEM((2 * HALF_BLKS, BLK, HD), jnp.bfloat16),
            pltpu.VMEM((2 * HALF_BLKS, HD, BLK), jnp.bfloat16),
            pltpu.VMEM((2 * HALF_BLKS, HD, BLK), jnp.bfloat16),
            pltpu.VMEM((HALF_BLKS + 1, BLK, COLS), jnp.float32),
            pltpu.VMEM((2 * HALF_BLKS, BLK, HD), jnp.float32),
            pltpu.VMEM((2 * HALF_BLKS, BLK, HD), jnp.float32),
            pltpu.VMEM((HALF_BLKS, PAIR, 2 * GROUP, TOK, HD), jnp.bfloat16),
            pltpu.VMEM((PEERS, 2, TOK, HD), jnp.bfloat16),
            pltpu.SemaphoreType.DMA((HALF_BLKS,)),
            pltpu.SemaphoreType.DMA,
        ],
        compiler_params=pltpu.CompilerParams(vmem_limit_bytes=24 * 1024 * 1024),
        name="attend_half",
    )(info, qd, kv, halo, starts)


def doc_reach(doc_lengths, half_index):
    before = lax.broadcasted_iota(jnp.int32, (128, 128), 0) <= lax.broadcasted_iota(jnp.int32, (128, 128), 1)
    ends = jnp.sum(jnp.where(before, doc_lengths[:, None], 0), axis=0)
    positions = half_index * HALF + jnp.arange(HALF, dtype=jnp.int32)
    begins = jnp.max(jnp.where(ends[None, :] <= positions[:, None], ends[None, :], 0), axis=1)
    begins = (begins - (half_index - 1) * HALF).reshape(HALF_BLKS, 1, BLK)
    low = begins[:, 0, 0] // BLK
    return jnp.concatenate([begins] * GROUP, axis=2), low


def pieces(width):
    for peer in range(PEERS):
        for place in range(width):
            yield peer, place, pl.ds((peer * width + place) * HD, HD)


def pack_kernel(width, first, second, out):
    for peer, place, columns in pieces(width):
        out[peer, place] = first[:, columns]
        out[peer, width + place] = second[:, columns]


def packed(first, second, width):
    in_vmem = pl.BlockSpec(memory_space=pltpu.VMEM)
    return pl.pallas_call(
        functools.partial(pack_kernel, width),
        out_shape=jax.ShapeDtypeStruct((PEERS, 2 * width, TOK, HD), jnp.bfloat16),
        in_specs=[in_vmem, in_vmem],
        out_specs=in_vmem,
        compiler_params=pltpu.CompilerParams(vmem_limit_bytes=8 * 1024 * 1024) if width > 1 else None,
        name="pack_heads",
    )(first, second)


def unpack_kernel(width, array, first, second):
    for peer, place, columns in pieces(width):
        first[:, columns] = array[peer, place]
        second[:, columns] = array[peer, width + place]


def unpacked(array, width):
    in_vmem = pl.BlockSpec(memory_space=pltpu.VMEM)
    rows = jax.ShapeDtypeStruct((TOK, PEERS * width * HD), jnp.bfloat16)
    return pl.pallas_call(
        functools.partial(unpack_kernel, width),
        out_shape=(rows, rows),
        in_specs=[in_vmem],
        out_specs=(in_vmem, in_vmem),
        compiler_params=pltpu.CompilerParams(vmem_limit_bytes=8 * 1024 * 1024),
        name="unpack_heads",
    )(array)


def join_kernel(own, back, out):
    out[...] = (own[...] + back[...].astype(jnp.float32)).astype(jnp.bfloat16)


def joined(own, back):
    in_vmem = pl.BlockSpec(memory_space=pltpu.VMEM)
    return pl.pallas_call(
        join_kernel,
        out_shape=jax.ShapeDtypeStruct(back.shape, jnp.bfloat16),
        in_specs=[in_vmem, in_vmem],
        out_specs=in_vmem,
        compiler_params=pltpu.CompilerParams(vmem_limit_bytes=8 * 1024 * 1024),
        cost_estimate=pl.CostEstimate(flops=30_000_000_000, bytes_accessed=100_000_000, transcendentals=0),
        name="join_grads",
    )(own, back)


def on_device(queries, keys, values, grad_out, doc_lengths):
    ahead = next_half_pairs(lax.axis_size("dp"))
    behind = [(to, of) for of, to in ahead]
    both = ("dp", "ctx")
    half = lax.axis_index("ctx") // PEERS
    starts, low = doc_reach(doc_lengths, lax.axis_index("dp") * 2 + half)
    info = jnp.concatenate([half[None].astype(jnp.int32), low])

    kv = exchange(packed(keys, values, 1))
    halo = lax.ppermute(kv, both, ahead)
    queries, grad_out, starts, info = lax.optimization_barrier((queries, grad_out, starts, info))
    qd = exchange(packed(queries, grad_out, GROUP))
    od, own_grads, halo_grads = attend_half(info, qd, kv, halo, starts)
    back = lax.ppermute(halo_grads, both, behind)
    attended, grad_queries = unpacked(exchange(od), GROUP)
    grads = joined(own_grads, back)
    grad_keys, grad_values = unpacked(exchange(grads), 1)
    return attended, grad_queries, grad_keys, grad_values


def solution(mesh):
    rows = P(("dp", "ctx"), None)
    return jax.shard_map(
        on_device, mesh=mesh, in_specs=(rows, rows, rows, rows, P()), out_specs=(rows,) * 4, check_vma=False
    )
```

```python
import functools

import jax
import jax.numpy as jnp
from jax import lax
from jax.experimental import pallas as pl
from jax.experimental.pallas import tpu as pltpu
from jax.sharding import PartitionSpec as P

HEADS = 16
KV_HEADS = 8
HD = 128
GROUP = HEADS // KV_HEADS

TOK = 128
PEERS = 8
HALF = TOK * PEERS
BLK = 256
HALF_BLKS = HALF // BLK
PAIR = BLK // TOK
COLS = GROUP * BLK

q_scale = 144.0 ** (-0.5)
log2_e = 1.4426950408889634
far_below = -1e30

OWNERS = ((0, 1, 2, 3, 4, 5, 6, 7), (12, 13, 14, 15, 8, 9, 10, 11))


def exchange(array):
    return lax.all_to_all(
        array, "ctx", split_axis=0, concat_axis=0, tiled=True, axis_index_groups=[list(g) for g in OWNERS]
    )


def next_half_pairs(rows):
    pairs = []
    for row in range(rows):
        for first, second in zip(*OWNERS):
            pairs.append((row * 16 + first, row * 16 + second))
            if row + 1 < rows:
                pairs.append((row * 16 + second, (row + 1) * 16 + first))
    return pairs


def nt(left, right):
    return lax.dot_general(left, right, (((1,), (1,)), ((), ())), preferred_element_type=jnp.float32)


def nn(left, right):
    return lax.dot_general(left, right, (((1,), (0,)), ((), ())), preferred_element_type=jnp.float32)


def fold(array, op):
    return op(array.reshape(BLK // 8, 8, COLS), axis=0)


def attend_kernel(
    info, qd, kv, halo, starts, od, own_grads, halo_grads,
    k_rows, v_rows, k_cols, v_cols, held, key_grads, value_grads, od_rows, halo_rows, od_sems, halo_sem,
):
    half = info[0]

    def own_at(block):
        return lax.rem(block + half * (HALF_BLKS // 2), HALF_BLKS) * PAIR

    def halo_at(block):
        return lax.rem(block + (1 - half) * (HALF_BLKS // 2), HALF_BLKS) * PAIR

    for block in range(HALF_BLKS):
        for ref, at, first in ((halo, halo_at, 0), (kv, own_at, HALF_BLKS)):
            k_blk = ref[pl.ds(at(block), PAIR), 0].reshape(BLK, HD)
            v_blk = ref[pl.ds(at(block), PAIR), 1].reshape(BLK, HD)
            k_rows[first + block] = k_blk
            v_rows[first + block] = v_blk
            k_cols[first + block] = k_blk.T
            v_cols[first + block] = v_blk.T
    for sums in (key_grads, value_grads):
        sums[:HALF_BLKS] = jnp.zeros((HALF_BLKS, BLK, HD), jnp.float32)

    def attend(block, count):
        q_at = pl.ds(own_at(block), PAIR)
        q_blk = jnp.concatenate([qd[q_at, 0].reshape(BLK, HD), qd[q_at, 1].reshape(BLK, HD)], axis=0)
        d_blk = jnp.concatenate([qd[q_at, 2].reshape(BLK, HD), qd[q_at, 3].reshape(BLK, HD)], axis=0)
        q_cols = q_blk.T
        d_cols = d_blk.T
        start = starts[block]
        low = HALF_BLKS + block + 1 - count
        highest = None
        for step in range(count):
            piece = nn(k_rows[low + step], q_cols)
            at = lax.broadcasted_iota(jnp.int32, (BLK, COLS), 0)
            allowed = at >= start - (low + step) * BLK
            if step == count - 1:
                q_pos = lax.rem(lax.broadcasted_iota(jnp.int32, (BLK, COLS), 1), BLK)
                allowed = allowed & (at <= q_pos)
            piece = jnp.where(allowed, piece, far_below)
            held[step] = piece
            best = fold(piece, jnp.max)
            highest = best if highest is None else jnp.maximum(highest, best)
        highest = jnp.max(highest, axis=0, keepdims=True) * (q_scale * log2_e)
        summed = mixture = 0.0
        for step in range(count):
            piece = jnp.exp2(held[step] * (q_scale * log2_e) - highest)
            held[step] = piece
            summed = summed + fold(piece, jnp.sum)
            mixture = mixture + nn(v_cols[low + step], piece.astype(jnp.bfloat16))
        inverse = 1.0 / jnp.sum(summed, axis=0, keepdims=True)
        attended = (mixture * inverse).astype(jnp.bfloat16)
        row_delta = jnp.sum(
            attended.astype(jnp.float32) * d_cols.astype(jnp.float32), axis=0, keepdims=True
        )
        out_rows = attended.T
        od_rows[block, :, 0] = out_rows[:BLK].reshape(PAIR, TOK, HD)
        od_rows[block, :, 1] = out_rows[BLK:].reshape(PAIR, TOK, HD)
        grad_q = 0.0
        for step in range(count):
            weights = held[step] * inverse
            dscore = (weights * (nn(v_rows[low + step], d_cols) - row_delta)).astype(jnp.bfloat16)
            value_part = nn(weights.astype(jnp.bfloat16), d_blk)
            key_part = nn(dscore, q_blk)
            if step == count - 1:
                value_grads[low + step] = value_part
                key_grads[low + step] = key_part
            else:
                value_grads[low + step] += value_part
                key_grads[low + step] += key_part
            grad_q = grad_q + nn(k_cols[low + step], dscore)
        out_rows = (grad_q * q_scale).astype(jnp.bfloat16).T
        od_rows[block, :, 2] = out_rows[:BLK].reshape(PAIR, TOK, HD)
        od_rows[block, :, 3] = out_rows[BLK:].reshape(PAIR, TOK, HD)

    def od_copy(block):
        return pltpu.make_async_copy(od_rows.at[block], od.at[pl.ds(own_at(block), PAIR)], od_sems.at[block])

    @pl.loop(0, HALF_BLKS)
    def _(block):
        count = HALF_BLKS + block + 1 - info[1 + block]
        for choice in range(1, HALF_BLKS + 2):
            pl.when(count == choice)(lambda choice=choice: attend(block, choice))
        od_copy(block).start()

    for block in range(HALF_BLKS):
        at_pair = pl.ds(halo_at(block), PAIR)
        halo_rows[at_pair, 0] = (key_grads[block] * q_scale).astype(jnp.bfloat16).reshape(PAIR, TOK, HD)
        halo_rows[at_pair, 1] = value_grads[block].astype(jnp.bfloat16).reshape(PAIR, TOK, HD)
    halo_copy = pltpu.make_async_copy(halo_rows, halo_grads, halo_sem)
    halo_copy.start()
    for block in range(HALF_BLKS):
        at_pair = pl.ds(own_at(block), PAIR)
        own_grads[at_pair, 0] = (key_grads[HALF_BLKS + block] * q_scale).astype(jnp.bfloat16).reshape(PAIR, TOK, HD)
        own_grads[at_pair, 1] = value_grads[HALF_BLKS + block].astype(jnp.bfloat16).reshape(PAIR, TOK, HD)
    for block in range(HALF_BLKS):
        od_copy(block).wait()
    halo_copy.wait()


def attend_half(info, qd, kv, halo, starts):
    in_vmem = pl.BlockSpec(memory_space=pltpu.VMEM)
    in_hbm = pl.BlockSpec(memory_space=pltpu.HBM)
    return pl.pallas_call(
        attend_kernel,
        out_shape=(
            pltpu.HBM((PEERS, 2 * GROUP, TOK, HD), jnp.bfloat16),
            jax.ShapeDtypeStruct((PEERS, 2, TOK, HD), jnp.bfloat16),
            pltpu.HBM((PEERS, 2, TOK, HD), jnp.bfloat16),
        ),
        in_specs=[pl.BlockSpec(memory_space=pltpu.SMEM)] + [in_vmem] * 4,
        out_specs=(in_hbm, in_vmem, in_hbm),
        scratch_shapes=[
            pltpu.VMEM((2 * HALF_BLKS, BLK, HD), jnp.bfloat16),
            pltpu.VMEM((2 * HALF_BLKS, BLK, HD), jnp.bfloat16),
            pltpu.VMEM((2 * HALF_BLKS, HD, BLK), jnp.bfloat16),
            pltpu.VMEM((2 * HALF_BLKS, HD, BLK), jnp.bfloat16),
            pltpu.VMEM((HALF_BLKS + 1, BLK, COLS), jnp.float32),
            pltpu.VMEM((2 * HALF_BLKS, BLK, HD), jnp.float32),
            pltpu.VMEM((2 * HALF_BLKS, BLK, HD), jnp.float32),
            pltpu.VMEM((HALF_BLKS, PAIR, 2 * GROUP, TOK, HD), jnp.bfloat16),
            pltpu.VMEM((PEERS, 2, TOK, HD), jnp.bfloat16),
            pltpu.SemaphoreType.DMA((HALF_BLKS,)),
            pltpu.SemaphoreType.DMA,
        ],
        compiler_params=pltpu.CompilerParams(vmem_limit_bytes=24 * 1024 * 1024),
        name="attend_half",
    )(info, qd, kv, halo, starts)


def doc_reach(doc_lengths, half_index):
    before = lax.broadcasted_iota(jnp.int32, (128, 128), 0) <= lax.broadcasted_iota(jnp.int32, (128, 128), 1)
    ends = jnp.sum(jnp.where(before, doc_lengths[:, None], 0), axis=0)
    positions = half_index * HALF + jnp.arange(HALF, dtype=jnp.int32)
    begins = jnp.max(jnp.where(ends[None, :] <= positions[:, None], ends[None, :], 0), axis=1)
    begins = (begins - (half_index - 1) * HALF).reshape(HALF_BLKS, 1, BLK)
    low = begins[:, 0, 0] // BLK
    return jnp.concatenate([begins] * GROUP, axis=2), low


def pieces(width):
    for peer in range(PEERS):
        for place in range(width):
            yield peer, place, pl.ds((peer * width + place) * HD, HD)


def pack_kernel(width, first, second, out):
    for peer, place, columns in pieces(width):
        out[peer, place] = first[:, columns]
        out[peer, width + place] = second[:, columns]


def packed(first, second, width):
    in_vmem = pl.BlockSpec(memory_space=pltpu.VMEM)
    return pl.pallas_call(
        functools.partial(pack_kernel, width),
        out_shape=jax.ShapeDtypeStruct((PEERS, 2 * width, TOK, HD), jnp.bfloat16),
        in_specs=[in_vmem, in_vmem],
        out_specs=in_vmem,
        compiler_params=pltpu.CompilerParams(vmem_limit_bytes=8 * 1024 * 1024) if width > 1 else None,
        name="pack_heads",
    )(first, second)


def unpack_kernel(width, array, first, second):
    for peer, place, columns in pieces(width):
        first[:, columns] = array[peer, place]
        second[:, columns] = array[peer, width + place]


def unpacked(array, width):
    in_vmem = pl.BlockSpec(memory_space=pltpu.VMEM)
    rows = jax.ShapeDtypeStruct((TOK, PEERS * width * HD), jnp.bfloat16)
    return pl.pallas_call(
        functools.partial(unpack_kernel, width),
        out_shape=(rows, rows),
        in_specs=[in_vmem],
        out_specs=(in_vmem, in_vmem),
        compiler_params=pltpu.CompilerParams(vmem_limit_bytes=8 * 1024 * 1024),
        name="unpack_heads",
    )(array)


def join_kernel(own, back, out):
    out[...] = (own[...].astype(jnp.float32) + back[...].astype(jnp.float32)).astype(jnp.bfloat16)


def joined(own, back):
    in_vmem = pl.BlockSpec(memory_space=pltpu.VMEM)
    return pl.pallas_call(
        join_kernel,
        out_shape=jax.ShapeDtypeStruct(back.shape, jnp.bfloat16),
        in_specs=[in_vmem, in_vmem],
        out_specs=in_vmem,
        compiler_params=pltpu.CompilerParams(vmem_limit_bytes=8 * 1024 * 1024),
        cost_estimate=pl.CostEstimate(flops=30_000_000_000, bytes_accessed=100_000_000, transcendentals=0),
        name="join_grads",
    )(own, back)


def on_device(queries, keys, values, grad_out, doc_lengths):
    ahead = next_half_pairs(lax.axis_size("dp"))
    behind = [(to, of) for of, to in ahead]
    both = ("dp", "ctx")
    half = lax.axis_index("ctx") // PEERS
    starts, low = doc_reach(doc_lengths, lax.axis_index("dp") * 2 + half)
    info = jnp.concatenate([half[None].astype(jnp.int32), low])

    kv = exchange(packed(keys, values, 1))
    halo = lax.ppermute(kv, both, ahead)
    queries, grad_out, starts, info = lax.optimization_barrier((queries, grad_out, starts, info))
    qd = exchange(packed(queries, grad_out, GROUP))
    od, own_grads, halo_grads = attend_half(info, qd, kv, halo, starts)
    back = lax.ppermute(halo_grads, both, behind)
    attended, grad_queries = unpacked(exchange(od), GROUP)
    grads = joined(own_grads, back)
    grad_keys, grad_values = unpacked(exchange(grads), 1)
    return attended, grad_queries, grad_keys, grad_values


def solution(mesh):
    rows = P(("dp", "ctx"), None)
    return jax.shard_map(
        on_device, mesh=mesh, in_specs=(rows, rows, rows, rows, P()), out_specs=(rows,) * 4, check_vma=False
    )
```

```python
import functools

import jax
import jax.numpy as jnp
from jax import lax
from jax.experimental import pallas as pl
from jax.experimental.pallas import tpu as pltpu
from jax.sharding import PartitionSpec as P

HEADS = 16
KV_HEADS = 8
HD = 128
GROUP = HEADS // KV_HEADS

TOK = 128
PEERS = 8
HALF = TOK * PEERS
BLK = 256
HALF_BLKS = HALF // BLK
PAIR = BLK // TOK
COLS = GROUP * BLK

q_scale = 144.0 ** (-0.5)
log2_e = 1.4426950408889634
far_below = -1e30

OWNERS = ((0, 1, 2, 3, 4, 5, 6, 7), (12, 13, 14, 15, 8, 9, 10, 11))


def exchange(array):
    return lax.all_to_all(
        array, "ctx", split_axis=0, concat_axis=0, tiled=True, axis_index_groups=[list(g) for g in OWNERS]
    )


def next_half_pairs(rows):
    pairs = []
    for row in range(rows):
        for first, second in zip(*OWNERS):
            pairs.append((row * 16 + first, row * 16 + second))
            if row + 1 < rows:
                pairs.append((row * 16 + second, (row + 1) * 16 + first))
    return pairs


def nt(left, right):
    return lax.dot_general(left, right, (((1,), (1,)), ((), ())), preferred_element_type=jnp.float32)


def nn(left, right):
    return lax.dot_general(left, right, (((1,), (0,)), ((), ())), preferred_element_type=jnp.float32)


def fold(array, op):
    return op(array.reshape(BLK // 8, 8, COLS), axis=0)


def attend_kernel(
    info, qd, kv, halo, starts, od, own_grads, halo_grads,
    k_rows, v_rows, k_cols, v_cols, held, key_grads, value_grads, od_rows, halo_rows, od_sems, halo_sem,
):
    half = info[0]

    def own_at(block):
        return lax.rem(block + half * (HALF_BLKS // 2), HALF_BLKS) * PAIR

    def halo_at(block):
        return lax.rem(block + (1 - half) * (HALF_BLKS // 2), HALF_BLKS) * PAIR

    def prepare(ref, at, place):
        k_blk = ref[pl.ds(at, PAIR), 0].reshape(BLK, HD)
        v_blk = ref[pl.ds(at, PAIR), 1].reshape(BLK, HD)
        k_rows[place] = k_blk
        v_rows[place] = v_blk
        k_cols[place] = k_blk.T
        v_cols[place] = v_blk.T

    for block in range(HALF_BLKS):
        prepare(kv, own_at(block), HALF_BLKS + block)
        pl.when(block >= info[1])(lambda block=block: prepare(halo, halo_at(block), block))
    for sums in (key_grads, value_grads):
        sums[:HALF_BLKS] = jnp.zeros((HALF_BLKS, BLK, HD), jnp.float32)

    def attend(block, count):
        q_at = pl.ds(own_at(block), PAIR)
        q_blk = jnp.concatenate([qd[q_at, 0].reshape(BLK, HD), qd[q_at, 1].reshape(BLK, HD)], axis=0)
        d_blk = jnp.concatenate([qd[q_at, 2].reshape(BLK, HD), qd[q_at, 3].reshape(BLK, HD)], axis=0)
        q_cols = q_blk.T
        d_cols = d_blk.T
        start = starts[block]
        low = HALF_BLKS + block + 1 - count
        highest = None
        for step in range(count):
            piece = nn(k_rows[low + step], q_cols)
            at = lax.broadcasted_iota(jnp.int32, (BLK, COLS), 0)
            allowed = at >= start - (low + step) * BLK
            if step == count - 1:
                q_pos = lax.rem(lax.broadcasted_iota(jnp.int32, (BLK, COLS), 1), BLK)
                allowed = allowed & (at <= q_pos)
            piece = jnp.where(allowed, piece, far_below)
            held[step] = piece
            best = fold(piece, jnp.max)
            highest = best if highest is None else jnp.maximum(highest, best)
        highest = jnp.max(highest, axis=0, keepdims=True) * (q_scale * log2_e)
        summed = mixture = 0.0
        for step in range(count):
            piece = jnp.exp2(held[step] * (q_scale * log2_e) - highest)
            held[step] = piece
            summed = summed + fold(piece, jnp.sum)
            mixture = mixture + nn(v_cols[low + step], piece.astype(jnp.bfloat16))
        inverse = 1.0 / jnp.sum(summed, axis=0, keepdims=True)
        attended = (mixture * inverse).astype(jnp.bfloat16)
        row_delta = jnp.sum(
            attended.astype(jnp.float32) * d_cols.astype(jnp.float32), axis=0, keepdims=True
        )
        out_rows = attended.T
        od_rows[block, :, 0] = out_rows[:BLK].reshape(PAIR, TOK, HD)
        od_rows[block, :, 1] = out_rows[BLK:].reshape(PAIR, TOK, HD)
        grad_q = 0.0
        for step in range(count):
            weights = held[step] * inverse
            dscore = (weights * (nn(v_rows[low + step], d_cols) - row_delta)).astype(jnp.bfloat16)
            value_part = nn(weights.astype(jnp.bfloat16), d_blk)
            key_part = nn(dscore, q_blk)
            if step == count - 1:
                value_grads[low + step] = value_part
                key_grads[low + step] = key_part
            else:
                value_grads[low + step] += value_part
                key_grads[low + step] += key_part
            grad_q = grad_q + nn(k_cols[low + step], dscore)
        out_rows = (grad_q * q_scale).astype(jnp.bfloat16).T
        od_rows[block, :, 2] = out_rows[:BLK].reshape(PAIR, TOK, HD)
        od_rows[block, :, 3] = out_rows[BLK:].reshape(PAIR, TOK, HD)

    def od_copy(block):
        return pltpu.make_async_copy(od_rows.at[block], od.at[pl.ds(own_at(block), PAIR)], od_sems.at[block])

    @pl.loop(0, HALF_BLKS)
    def _(block):
        count = HALF_BLKS + block + 1 - info[1 + block]
        for choice in range(1, HALF_BLKS + 2):
            pl.when(count == choice)(lambda choice=choice: attend(block, choice))
        od_copy(block).start()

    for block in range(HALF_BLKS):
        at_pair = pl.ds(halo_at(block), PAIR)
        halo_rows[at_pair, 0] = (key_grads[block] * q_scale).astype(jnp.bfloat16).reshape(PAIR, TOK, HD)
        halo_rows[at_pair, 1] = value_grads[block].astype(jnp.bfloat16).reshape(PAIR, TOK, HD)
    halo_copy = pltpu.make_async_copy(halo_rows, halo_grads, halo_sem)
    halo_copy.start()
    for block in range(HALF_BLKS):
        at_pair = pl.ds(own_at(block), PAIR)
        own_grads[at_pair, 0] = (key_grads[HALF_BLKS + block] * q_scale).reshape(PAIR, TOK, HD)
        own_grads[at_pair, 1] = value_grads[HALF_BLKS + block].reshape(PAIR, TOK, HD)
    for block in range(HALF_BLKS):
        od_copy(block).wait()
    halo_copy.wait()


def attend_half(info, qd, kv, halo, starts):
    in_vmem = pl.BlockSpec(memory_space=pltpu.VMEM)
    in_hbm = pl.BlockSpec(memory_space=pltpu.HBM)
    return pl.pallas_call(
        attend_kernel,
        out_shape=(
            pltpu.HBM((PEERS, 2 * GROUP, TOK, HD), jnp.bfloat16),
            jax.ShapeDtypeStruct((PEERS, 2, TOK, HD), jnp.float32),
            pltpu.HBM((PEERS, 2, TOK, HD), jnp.bfloat16),
        ),
        in_specs=[pl.BlockSpec(memory_space=pltpu.SMEM)] + [in_vmem] * 4,
        out_specs=(in_hbm, in_vmem, in_hbm),
        scratch_shapes=[
            pltpu.VMEM((2 * HALF_BLKS, BLK, HD), jnp.bfloat16),
            pltpu.VMEM((2 * HALF_BLKS, BLK, HD), jnp.bfloat16),
            pltpu.VMEM((2 * HALF_BLKS, HD, BLK), jnp.bfloat16),
            pltpu.VMEM((2 * HALF_BLKS, HD, BLK), jnp.bfloat16),
            pltpu.VMEM((HALF_BLKS + 1, BLK, COLS), jnp.float32),
            pltpu.VMEM((2 * HALF_BLKS, BLK, HD), jnp.float32),
            pltpu.VMEM((2 * HALF_BLKS, BLK, HD), jnp.float32),
            pltpu.VMEM((HALF_BLKS, PAIR, 2 * GROUP, TOK, HD), jnp.bfloat16),
            pltpu.VMEM((PEERS, 2, TOK, HD), jnp.bfloat16),
            pltpu.SemaphoreType.DMA((HALF_BLKS,)),
            pltpu.SemaphoreType.DMA,
        ],
        compiler_params=pltpu.CompilerParams(vmem_limit_bytes=24 * 1024 * 1024),
        name="attend_half",
    )(info, qd, kv, halo, starts)


def doc_reach(doc_lengths, half_index):
    before = lax.broadcasted_iota(jnp.int32, (128, 128), 0) <= lax.broadcasted_iota(jnp.int32, (128, 128), 1)
    ends = jnp.sum(jnp.where(before, doc_lengths[:, None], 0), axis=0)
    positions = half_index * HALF + jnp.arange(HALF, dtype=jnp.int32)
    begins = jnp.max(jnp.where(ends[None, :] <= positions[:, None], ends[None, :], 0), axis=1)
    begins = (begins - (half_index - 1) * HALF).reshape(HALF_BLKS, 1, BLK)
    low = begins[:, 0, 0] // BLK
    return jnp.concatenate([begins] * GROUP, axis=2), low


def pieces(width):
    for peer in range(PEERS):
        for place in range(width):
            yield peer, place, pl.ds((peer * width + place) * HD, HD)


def pack_kernel(width, first, second, out):
    for peer, place, columns in pieces(width):
        out[peer, place] = first[:, columns]
        out[peer, width + place] = second[:, columns]


def packed(first, second, width):
    in_vmem = pl.BlockSpec(memory_space=pltpu.VMEM)
    return pl.pallas_call(
        functools.partial(pack_kernel, width),
        out_shape=jax.ShapeDtypeStruct((PEERS, 2 * width, TOK, HD), jnp.bfloat16),
        in_specs=[in_vmem, in_vmem],
        out_specs=in_vmem,
        compiler_params=pltpu.CompilerParams(vmem_limit_bytes=8 * 1024 * 1024) if width > 1 else None,
        name="pack_heads",
    )(first, second)


def unpack_kernel(width, array, first, second):
    for peer, place, columns in pieces(width):
        first[:, columns] = array[peer, place]
        second[:, columns] = array[peer, width + place]


def unpacked(array, width):
    in_vmem = pl.BlockSpec(memory_space=pltpu.VMEM)
    rows = jax.ShapeDtypeStruct((TOK, PEERS * width * HD), jnp.bfloat16)
    return pl.pallas_call(
        functools.partial(unpack_kernel, width),
        out_shape=(rows, rows),
        in_specs=[in_vmem],
        out_specs=(in_vmem, in_vmem),
        compiler_params=pltpu.CompilerParams(vmem_limit_bytes=8 * 1024 * 1024),
        name="unpack_heads",
    )(array)


def join_kernel(own, back, out):
    out[...] = (own[...] + back[...].astype(jnp.float32)).astype(jnp.bfloat16)


def joined(own, back):
    in_vmem = pl.BlockSpec(memory_space=pltpu.VMEM)
    return pl.pallas_call(
        join_kernel,
        out_shape=jax.ShapeDtypeStruct(back.shape, jnp.bfloat16),
        in_specs=[in_vmem, in_vmem],
        out_specs=in_vmem,
        compiler_params=pltpu.CompilerParams(vmem_limit_bytes=8 * 1024 * 1024),
        cost_estimate=pl.CostEstimate(flops=30_000_000_000, bytes_accessed=100_000_000, transcendentals=0),
        name="join_grads",
    )(own, back)


def on_device(queries, keys, values, grad_out, doc_lengths):
    ahead = next_half_pairs(lax.axis_size("dp"))
    behind = [(to, of) for of, to in ahead]
    both = ("dp", "ctx")
    half = lax.axis_index("ctx") // PEERS
    starts, low = doc_reach(doc_lengths, lax.axis_index("dp") * 2 + half)
    info = jnp.concatenate([half[None].astype(jnp.int32), low])

    kv = exchange(packed(keys, values, 1))
    halo = lax.ppermute(kv, both, ahead)
    queries, grad_out, starts, info = lax.optimization_barrier((queries, grad_out, starts, info))
    qd = exchange(packed(queries, grad_out, GROUP))
    od, own_grads, halo_grads = attend_half(info, qd, kv, halo, starts)
    back = lax.ppermute(halo_grads, both, behind)
    attended, grad_queries = unpacked(exchange(od), GROUP)
    grads = joined(own_grads, back)
    grad_keys, grad_values = unpacked(exchange(grads), 1)
    return attended, grad_queries, grad_keys, grad_values


def solution(mesh):
    rows = P(("dp", "ctx"), None)
    return jax.shard_map(
        on_device, mesh=mesh, in_specs=(rows, rows, rows, rows, P()), out_specs=(rows,) * 4, check_vma=False
    )
```
